128 devices in a mesh: elem: 8 (over z, y_lo), snap: 16 (over x, y_hi, core).
Axes of the slice: x: 4, y: 4 (y_hi: 2, y_lo: 2; y = y_hi * 2 + y_lo), z: 4, core: 2. Of those that a mesh axis runs over, the one named last changes fastest.
Arguments:
- snapshots: bfloat16 [2048, 6, 65536], P('snap', None, 'elem'), may hold values from -6 to 6
- coefficients: bfloat16 [2048, 128], P('snap'), may hold values from -0.125 to 0.125
- mass_weights: float32 [65536], P('elem'), may hold values from 3.90625e-05 to 0.000390625
- metric: float32 [3, 3, 65536], P(None, None, 'elem'), may hold values from -3 to 3
- out_modes: int32 [32], replicated, may hold values from 0 to 127, as said below
Outputs:
- tensor: float32 [32, 128, 128], P(None, 'snap', 'elem')
- diffusion: float32 [32, 128], P('elem', 'snap')
The draws below stay inside these ranges and needn't reach their ends.
Inputs may be any that keep to these rules, and one draw needn't show every extreme that they name: `out_modes`: 32 distinct mode numbers; 0 and 127 are always among them.
All inputs are finite; a program needn't handle non-finite values.
Results may differ from the reference program's by a relative error of at most 0.035.
Values may be sent and summed in bfloat16 or wider, within the bound.
No kernel may reach another device: no remote copies, remote signals or barrier semaphores. Data moves between devices by JAX's collectives and lax.ppermute only.
A program may use at most 256 MiB of HBM per device.

```python
import math
import jax
import jax.numpy as jnp
import numpy as np
from jax import lax

GLL = 8
NPE = 512
MODES = 128
OUT = 32
SNAPS = 2048
NODES = 65536
N_SNAP = 16


def draw_out_modes(key, part):
    key = jax.random.fold_in(key, 7)
    middle = jax.random.permutation(key, MODES - 2)[:OUT - 2] + 1
    picked = jnp.concatenate([jnp.array([0], jnp.int32), middle.astype(jnp.int32), jnp.array([MODES - 1], jnp.int32)])
    return jax.random.permutation(jax.random.fold_in(key, 1), picked).astype(jnp.int32)


def block_levels(stream_key, shape, shards, low, largest):
    gain, own = 1.0, jax.random.fold_in(stream_key, 6)
    for position, blocks in shards:
        heights = jnp.exp(jax.random.uniform(jax.random.fold_in(own, position), (blocks,), jnp.float32, low / len(shards), largest / len(shards)))
        gain = gain * jnp.repeat(heights, shape[position] // blocks).reshape([-1 if axis == position else 1 for axis in range(len(shape))])
    return gain


def bell_draw(key, extent, spread, bound, cuts=(), held_as=jnp.bfloat16):
    factor_of = block_levels(key, extent, cuts, -0.22, 0.18) if cuts else 1.0
    values = jax.random.normal(key, extent, jnp.float32) * spread * factor_of
    return jnp.minimum(jnp.maximum(values, -bound), bound).astype(held_as)


def setup_inputs(seed: int = 0) -> dict:
    key_list = jax.random.split(jax.random.key(seed), 6)
    return {
        "snapshots": bell_draw(key_list[0], (SNAPS, 6, NODES), 1.0, 6.0, ((0, 16), (2, 8))),
        "coefficients": bell_draw(key_list[1], (SNAPS, MODES), SNAPS ** -0.5, 0.125, ((0, 16),)),
        "mass_weights": jnp.clip(jnp.exp(math.log(0.000390625) - 2.3025851 * jax.random.uniform(key_list[2], (NODES,), jnp.float32) ** block_levels(key_list[2], (NODES,), ((0, 8),), -0.2, 0.2)), 3.9062499126885086e-05, 0.000390625),
        "metric": bell_draw(key_list[3], (3, 3, NODES), 0.5, 3.0, ((2, 8),), jnp.float32),
        "out_modes": draw_out_modes(jax.random.fold_in(key_list[5], 71), 0),
    }


def legendre_pair(value, points):
    before, current = 1.0, value
    for degree in range(2, points):
        before, current = current, ((2 * degree - 1) * value * current - (degree - 1) * before) / degree
    return before, current


def derivative_tables(points):
    degree = points - 1
    nodes = [math.cos(math.pi * index / degree) for index in range(points)]
    for sweep in range(100):
        updated = []
        for value in nodes:
            before, current = legendre_pair(value, points)
            updated.append(value - (value * current - before) / (points * current))
        nodes = updated
    abscissae = sorted(nodes)
    evaluated = [legendre_pair(value, points)[1] for value in abscissae]
    matrix = np.zeros((points, points))
    for first in range(points):
        for second in range(points):
            if first != second:
                matrix[first, second] = evaluated[first] / (evaluated[second] * (abscissae[first] - abscissae[second]))
    matrix[0, 0] = -degree * (degree + 1) / 4.0
    matrix[degree, degree] = degree * (degree + 1) / 4.0
    identity = np.eye(points)
    stacked = np.stack([
        np.kron(identity, np.kron(identity, matrix.T)),
        np.kron(identity, np.kron(matrix.T, identity)),
        np.kron(matrix.T, np.kron(identity, identity)),
    ])
    return jnp.asarray(stacked, jnp.float32).astype(jnp.bfloat16)


def gradients(field, tables, metric):
    row_count, components, node_count = field.shape
    element_size = tables.shape[1]
    blocks = field.reshape(row_count * components * (node_count // element_size), element_size)
    accumulated = [jnp.zeros((row_count, components, node_count), jnp.float32) for target in range(3)]
    for direction in range(3):
        derived = jnp.dot(blocks, tables[direction], preferred_element_type=jnp.float32)
        derived = derived.reshape(row_count, components, node_count)
        for target in range(3):
            accumulated[target] = accumulated[target] + metric[direction, target] * derived
    return jnp.stack(accumulated, axis=2).astype(jnp.bfloat16)


def weighted_pairs(chosen, grads, weights):
    swapped = jnp.concatenate([chosen[:, 3:], chosen[:, :3]], axis=1)
    paired = jnp.stack([chosen.astype(jnp.float32), -swapped.astype(jnp.float32)], axis=0)
    product = jnp.einsum("pkax,jabx->kjpbx", paired, grads.astype(jnp.float32))
    return (product * weights).astype(jnp.bfloat16)


def diffusion_terms(grads_chosen, grads_all, weights):
    return jnp.einsum("kcbx,jcbx->kj", grads_chosen.astype(jnp.float32) * weights,
                      grads_all.astype(jnp.float32), precision=lax.Precision.HIGHEST)


def element_terms(phi_block, weights, metric_block, out_modes, tables):
    mode_count = phi_block.shape[0]
    out_count = out_modes.shape[0]
    grads_all = gradients(phi_block, tables, metric_block)
    chosen = phi_block[out_modes]
    grads_chosen = grads_all[out_modes]
    product = weighted_pairs(chosen, grads_all, weights).reshape(out_count * mode_count, -1)
    tensor = lax.dot_general(product, phi_block.reshape(mode_count, -1), (((1,), (1,)), ((), ())),
                             preferred_element_type=jnp.float32)
    tensor = tensor.reshape(out_count, mode_count, mode_count)
    return tensor, diffusion_terms(grads_chosen, grads_all, weights)


def reference(snapshots, coefficients, mass_weights, metric, out_modes):
    snap_total, components, node_total = snapshots.shape
    mode_count = coefficients.shape[1]
    out_count = out_modes.shape[0]
    group_rows = snap_total // N_SNAP
    snap_groups = snapshots.reshape(N_SNAP, group_rows, components * node_total)
    coef_groups = coefficients.reshape(N_SNAP, group_rows, mode_count)

    def add_group(accumulated, pieces):
        partial_value = lax.dot_general(pieces[1], pieces[0], (((0,), (0,)), ((), ())),
                                  preferred_element_type=jnp.float32)
        partial_value = lax.optimization_barrier(partial_value.astype(jnp.bfloat16)).astype(jnp.float32)
        return accumulated + partial_value, None

    summed, unused = lax.scan(add_group, jnp.zeros((mode_count, components * node_total), jnp.float32),
                              (snap_groups, coef_groups))
    modes = summed.astype(jnp.bfloat16).reshape(mode_count, components, node_total // NPE, NPE)
    modes = modes.transpose(2, 0, 1, 3)
    weights = mass_weights.reshape(node_total // NPE, NPE)
    metric_blocks = metric.reshape(3, 3, node_total // NPE, NPE).transpose(2, 0, 1, 3)
    tables = derivative_tables(GLL)

    def add_element(carry, pieces):
        tensor, diffusion = element_terms(pieces[0], pieces[1], pieces[2], out_modes, tables)
        return (carry[0] + tensor, carry[1] + diffusion), None

    start = (jnp.zeros((out_count, mode_count, mode_count), jnp.float32),
             jnp.zeros((out_count, mode_count), jnp.float32))
    totals, unused = lax.scan(add_element, start, (modes, weights, metric_blocks))
    return totals[0], totals[1]
```

```python
import math

import jax
import jax.numpy as jnp
import numpy as np
from jax import lax
from jax.experimental import pallas as pl
from jax.experimental.pallas import tpu as pltpu
from jax.sharding import PartitionSpec as P

GLL = 8
NPE = 512
AXES = ("elem", "snap")
BF = jnp.bfloat16
F32 = jnp.float32


def legendre_pair(value, points):
    before, current = (1.0, value)
    for degree in range(2, points):
        before, current = (
            current,
            ((2 * degree - 1) * value * current - (degree - 1) * before) / degree,
        )
    return (before, current)


def derivative_tables(points):
    degree = points - 1
    nodes = [math.cos(math.pi * index / degree) for index in range(points)]
    for sweep in range(100):
        updated = []
        for value in nodes:
            before, current = legendre_pair(value, points)
            updated.append(value - (value * current - before) / (points * current))
        nodes = updated
    abscissae = sorted(nodes)
    evaluated = [legendre_pair(value, points)[1] for value in abscissae]
    matrix = np.zeros((points, points))
    for first in range(points):
        for second in range(points):
            if first != second:
                matrix[first, second] = evaluated[first] / (
                    evaluated[second] * (abscissae[first] - abscissae[second])
                )
    matrix[0, 0] = -degree * (degree + 1) / 4.0
    matrix[degree, degree] = degree * (degree + 1) / 4.0
    identity = np.eye(points)
    stacked = np.concatenate(
        [
            np.kron(identity, np.kron(identity, matrix.T)),
            np.kron(identity, np.kron(matrix.T, identity)),
            np.kron(matrix.T, np.kron(identity, identity)),
        ],
        axis=1,
    )
    return jnp.asarray(stacked, jnp.float32).astype(jnp.bfloat16)


def place(x, y, z, core):
    return (z * 2 + y % 2) * 16 + (x * 2 + y // 2) * 2 + core


def moves(shift):
    pairs = []
    for x in range(4):
        for y in range(4):
            for z in range(4):
                for core in range(2):
                    nx, ny, nz, ncore = shift(x, y, z, core)
                    pairs.append((place(x, y, z, core), place(nx % 4, ny % 4, nz % 4, ncore)))
    return pairs


CORE = moves(lambda x, y, z, c: (x, y, z, 1 - c))
XP = moves(lambda x, y, z, c: (x + 1, y, z, c))
XM = moves(lambda x, y, z, c: (x - 1, y, z, c))
Y2 = moves(lambda x, y, z, c: (x, y + 2, z, c))


def send(value, pairs):
    return lax.ppermute(value, AXES, pairs)


ITEM = (3, 128, NPE)
ITEM_BYTES = 3 * 128 * NPE * 2
VMEM = 56 * 1024 * 1024


def item_cost(items, reads):
    return pl.CostEstimate(
        flops=2 * items * 3 * 128 * 128 * NPE,
        bytes_accessed=ITEM_BYTES * reads,
        transcendentals=0,
    )


def partials_kernel(ids, halves, coef_ref, x_ref, out_ref):
    coef = coef_ref[...].T
    for c in range(3):
        out_ref[0, c] = jnp.dot(coef, x_ref[c], preferred_element_type=F32).astype(BF)


def partials(fields, coef, ids, halves, name):
    count = len(ids)
    return pl.pallas_call(
        partials_kernel,
        grid_spec=pltpu.PrefetchScalarGridSpec(
            num_scalar_prefetch=2,
            grid=(count,),
            in_specs=[
                pl.BlockSpec((128, 128), lambda i, ids, halves: (0, 0)),
                pl.BlockSpec(ITEM, lambda i, ids, halves: (halves[i], 0, ids[i])),
            ],
            out_specs=pl.BlockSpec((1,) + ITEM, lambda i, ids, halves: (i, 0, 0, 0)),
        ),
        out_shape=jax.ShapeDtypeStruct((count,) + ITEM, BF),
        compiler_params=pltpu.CompilerParams(vmem_limit_bytes=VMEM),
        cost_estimate=item_cost(count, 2 * count),
        name=name,
    )(jnp.stack(ids), jnp.array(halves, jnp.int32), coef, fields)


def fixed(row):
    return lambda i, ids: (row, 0, 0, 0)


def sums(fields, coef, items, outs, name):
    plan, operands, specs = [], [], []
    for slot, (element, half, adds) in enumerate(items):
        operands.append(fields)
        specs.append(pl.BlockSpec(ITEM, lambda i, ids, slot=slot, half=half: (half, 0, ids[slot])))
    for element, half, adds in items:
        entry = []
        for array, row, span in adds:
            entry.append((len(operands), span))
            operands.append(array)
            specs.append(pl.BlockSpec((1,) + array.shape[1:], fixed(row)))
        plan.append(entry)

    def kernel(ids, coef_ref, *refs):
        ins, results = refs[: len(operands)], refs[len(operands) :]
        coef = coef_ref[...].T
        for slot, entry in enumerate(plan):
            for c in range(3):
                total = jnp.dot(coef, ins[slot][c], preferred_element_type=F32)
                whole = [position for position, span in entry if span is None]
                for position in whole:
                    total = total + ins[position][0, c].astype(F32)
                parts = {0: total[:64], 64: total[64:]}
                for position, span in entry:
                    if span is not None:
                        parts[span] = parts[span] + ins[position][0, c].astype(F32)
                for number, group in enumerate(outs):
                    for place_in, (item, span) in enumerate(group):
                        if item == slot and span is None:
                            results[number][place_in, c, :64] = parts[0].astype(BF)
                            results[number][place_in, c, 64:] = parts[64].astype(BF)
                        elif item == slot:
                            results[number][place_in, c] = parts[span].astype(BF)

    shapes = [(len(group), 3, 128 if group[0][1] is None else 64, NPE) for group in outs]
    return pl.pallas_call(
        kernel,
        grid_spec=pltpu.PrefetchScalarGridSpec(
            num_scalar_prefetch=1,
            grid=(1,),
            in_specs=[pl.BlockSpec((128, 128), lambda i, ids: (0, 0))] + specs,
            out_specs=[pl.BlockSpec(shape, lambda i, ids: (0, 0, 0, 0)) for shape in shapes],
        ),
        out_shape=[jax.ShapeDtypeStruct(shape, BF) for shape in shapes],
        compiler_params=pltpu.CompilerParams(vmem_limit_bytes=VMEM),
        cost_estimate=item_cost(len(items), len(operands) + len(items)),
        name=name,
    )(jnp.stack([element for element, half, adds in items]), coef, *operands)


KS = 34


def assemble_kernel(counts, ids, coef_ref, tables_ref, weight_ref, metric_ref, order_j, order_i, pick_k, pick_d,
                    xu_ref, xb_ref, *refs):
    adds_u, adds_b = refs[: counts[0]], refs[counts[0] : counts[0] + counts[1]]
    keep_ref, send_ref, zi_ref, zj_ref, g_ref, cb_ref = refs[counts[0] + counts[1] :]
    coef = coef_ref[...].T
    weight = weight_ref[...]
    half_weight = 0.5 * weight
    for a in range(3):
        u = jnp.dot(coef, xu_ref[a], preferred_element_type=F32)
        for ref in adds_u:
            u = u + ref[0, a].astype(F32)
        b = jnp.dot(coef, xb_ref[a], preferred_element_type=F32)
        for ref in adds_b:
            b = b + ref[0, a].astype(F32)
        for sign, z in ((0, u + b), (1, u - b)):
            z = z.astype(BF)
            zi_ref[:, ((1 - sign) * 3 + a) * NPE : ((1 - sign) * 3 + a + 1) * NPE] = jnp.dot(
                order_i[...], z, preferred_element_type=F32
            ).astype(BF)
            zj_ref[sign, a] = jnp.dot(order_j[...], z, preferred_element_type=F32).astype(BF)
            cb_ref[sign, a] = (
                jnp.dot(pick_k[...], z, preferred_element_type=F32) * half_weight
            ).astype(BF)

    diffusion = None
    for sign in range(2):
        for a in range(3):
            derived = jnp.dot(zj_ref[sign, a], tables_ref[...], preferred_element_type=F32)
            for b in range(3):
                grad = metric_ref[0, b : b + 1, :] * derived[:, :NPE]
                grad = grad + metric_ref[1, b : b + 1, :] * derived[:, NPE : 2 * NPE]
                grad = grad + metric_ref[2, b : b + 1, :] * derived[:, 2 * NPE :]
                grad = grad.astype(BF)
                g_ref[sign, a, b] = grad
                picked = jnp.dot(pick_d[...], grad, preferred_element_type=F32) * half_weight
                term = lax.dot_general(
                    grad, picked.astype(BF), (((1,), (1,)), ((), ())), preferred_element_type=F32
                )
                diffusion = term if diffusion is None else diffusion + term

    def put(k, block):
        block = block.astype(BF).reshape(2, 8, 8, 128)
        keep_ref[:, pl.ds(k, 1)] = block[0][:, None]
        send_ref[:, pl.ds(k, 1)] = block[1][:, None]

    put(32, diffusion)
    put(33, jnp.zeros((128, 128), F32))

    def row(k, carry):
        pieces = []
        for sign in range(2):
            picked = [cb_ref[sign, a, pl.ds(pl.multiple_of(k * 16, 16), 16), :][None] for a in range(3)]
            for b in range(3):
                total = None
                for a in range(3):
                    term = g_ref[sign, a, b].reshape(8, 16, NPE) * picked[a]
                    total = term if total is None else total + term
                pieces.append(total.reshape(128, NPE))
        product = jnp.concatenate(pieces, axis=1)
        put(k, lax.dot_general(product, zi_ref[...], (((1,), (1,)), ((), ())), preferred_element_type=F32))
        return carry

    lax.fori_loop(0, 32, row, 0)


def assemble(fields, coef, tables, weights, metric, order_j, order_i, pick_k, pick_d, element, adds_u, adds_b):
    def kernel(*args):
        assemble_kernel((len(adds_u), len(adds_b)), *args)

    def whole(shape):
        return pl.BlockSpec(shape, lambda i, ids: (0,) * len(shape))

    adds = adds_u + adds_b
    out = jax.ShapeDtypeStruct((8, KS, 8, 128), BF)
    return pl.pallas_call(
        kernel,
        grid_spec=pltpu.PrefetchScalarGridSpec(
            num_scalar_prefetch=1,
            grid=(1,),
            in_specs=[
                whole((128, 128)),
                whole(tables.shape),
                pl.BlockSpec((1, NPE), lambda i, ids: (0, ids[0])),
                pl.BlockSpec((3, 3, NPE), lambda i, ids: (0, 0, ids[0])),
                whole((128, 128)),
                whole((128, 128)),
                whole((512, 128)),
                whole((128, 128)),
                pl.BlockSpec(ITEM, lambda i, ids: (0, 0, ids[0])),
                pl.BlockSpec(ITEM, lambda i, ids: (1, 0, ids[0])),
            ]
            + [pl.BlockSpec((1,) + ITEM, fixed(row)) for array, row in adds],
            out_specs=[whole(out.shape), whole(out.shape)],
            scratch_shapes=[
                pltpu.VMEM((128, 6 * NPE), BF),
                pltpu.VMEM((2, 3, 128, NPE), BF),
                pltpu.VMEM((2, 3, 3, 128, NPE), BF),
                pltpu.VMEM((2, 3, 512, NPE), BF),
            ],
        ),
        out_shape=[out, out],
        compiler_params=pltpu.CompilerParams(vmem_limit_bytes=VMEM),
        cost_estimate=pl.CostEstimate(flops=10**10, bytes_accessed=10**7, transcendentals=0),
        name="assemble",
    )(element[None], coef, tables, weights, metric, order_j, order_i, pick_k, pick_d, fields, fields,
      *[array for array, row in adds])


def whole_call(kernel, outs, name, *operands):
    return pl.pallas_call(
        kernel,
        out_shape=outs,
        compiler_params=pltpu.CompilerParams(vmem_limit_bytes=VMEM),
        name=name,
    )(*operands)


def split_kernel(keep_ref, got_ref, *outs):
    for n in range(8):
        outs[n][...] = (keep_ref[n].astype(F32) + got_ref[n].astype(F32)).astype(BF)


def turn_kernel(*refs):
    ins, outs, rows = refs[:8], refs[8:16], refs[16]
    total = ins[0][...].astype(F32)
    for n in range(1, 8):
        total = total + ins[n][...].astype(F32)
    rows[...] = total.reshape(KS * 8, 128)
    ordered = [rows[pl.ds(j, 32, stride=8), :] for j in range(8)] + [rows[256:272, :]]
    turned = jnp.concatenate(ordered, axis=0).T
    for n in range(8):
        outs[n][...] = turned[n * 16 : n * 16 + 16].astype(BF)


def finish_kernel(*refs):
    ins, tensor_ref, diffusion_ref = refs[:8], refs[8], refs[9]
    total = ins[0][...].astype(F32)
    for n in range(1, 8):
        total = total + ins[n][...].astype(F32)
    for j in range(8):
        tensor_ref[j] = total[:, 32 * j : 32 * j + 32]
    diffusion_ref[...] = total[0:4, 256:264]


def on_device(snapshots, coefficients, mass_weights, metric, out_modes):
    fields = snapshots.transpose(1, 0, 2)
    snap, elem = lax.axis_index("snap"), lax.axis_index("elem")
    x, y_hi, core = snap // 4, (snap // 2) % 2, snap % 2
    z, y_lo = elem // 2, elem % 2

    def element(dx, dy, dcore=0):
        return ((core ^ dcore) * 8 + ((x + dx) % 4) * 2 + (y_hi ^ dy)).astype(jnp.int32)

    def exchange(wanted, name):
        ids = [element(dx, dy, 1) for half, dx, dy in wanted]
        value = partials(fields, coefficients, ids, [half for half, dx, dy in wanted], name)
        got = send(value, CORE)
        return {key: (got, n) for n, key in enumerate(wanted)}

    U, B = 0, 1
    got = exchange([(U, 2, 0), (U, 2, 1), (B, 2, 1)], "part1")
    got.update(exchange([(B, 1, 1), (B, 3, 1), (B, 0, 1)], "part2"))
    got.update(exchange([(U, 1, 1), (U, 3, 0), (U, 1, 0), (U, 3, 1)], "part3"))
    got.update(exchange([(U, 0, 1), (U, 0, 0), (B, 2, 0), (B, 1, 0), (B, 3, 0), (B, 0, 0)], "part4"))

    def item(half, dx, dy, *more):
        array, row = got[(half, dx, dy)]
        return (element(dx, dy), half, [(array, row, None)] + list(more))

    def total(items, outs, name):
        return sums(fields, coefficients, items, outs, name)

    one = [[(0, None)]]
    pair = [[(0, None)], [(1, None)]]
    both = [[(0, None), (1, None)]]
    yb1 = send(total([item(B, 2, 1)], one, "yb1")[0], Y2)
    right, left = total([item(U, 2, 0), item(U, 2, 1)], pair, "xa1")
    xa1r, xa1l = send(right, XP), send(left, XM)
    yb2 = send(total([item(B, 1, 1), item(B, 3, 1)], both, "yb2")[0], Y2)
    yb3 = send(total([item(B, 0, 1)], one, "yb3")[0], Y2)
    right, left = total([item(U, 1, 1), item(U, 3, 0)], pair, "xa2")
    xa2r, xa2l = send(right, XP), send(left, XM)
    right, left = total([item(U, 1, 0, (xa1r, 0, None)), item(U, 3, 1, (xa1l, 0, None))], pair, "xa3")
    xa3r, xa3l = send(right, XP), send(left, XM)
    right, left = total([item(B, 2, 0, (yb1, 0, None))], [[(0, 0)], [(0, 64)]], "xb1")
    xb1r, xb1l = send(right, XP), send(left, XM)
    right, left = total(
        [item(B, 1, 0, (yb2, 0, None), (xb1r, 0, 0)), item(B, 3, 0, (yb2, 1, None), (xb1l, 0, 64))], pair, "xb2"
    )
    xb2r, xb2l = send(right, XP), send(left, XM)
    ya = send(total([item(U, 0, 1, (xa2r, 0, None), (xa3l, 0, None))], one, "ya")[0], Y2)

    modes = lax.iota(jnp.int32, 128)
    part, offset = modes // 8, modes % 8
    order_j = ((((x + (part // 2) % 4) % 4) * 2 + (y_hi ^ (part % 2))) * 2 + (core ^ (part // 8))) * 8 + offset
    part, offset = modes // 16, modes % 16
    block = ((z + part // 2) % 4) * 2 + (y_lo ^ (part % 2))
    order_i = block * 16 + offset
    row = block * 4 + offset % 4
    picks = jnp.sum(jnp.where(row[:, None] == lax.iota(jnp.int32, 32)[None, :], out_modes[None, :], 0), axis=1)
    pick_d = ((picks[:, None] == order_j[None, :]) & (offset < 4)[:, None]).astype(BF)
    pick_k = (jnp.repeat(out_modes, 16)[:, None] == modes[None, :]).astype(BF)

    keep, out = assemble(
        fields, coefficients, derivative_tables(GLL), mass_weights.reshape(1, -1), metric,
        (order_j[:, None] == modes[None, :]).astype(BF), (order_i[:, None] == modes[None, :]).astype(BF),
        pick_k, pick_d, element(0, 0),
        [got[(U, 0, 0)], (xa2l, 0), (xa3r, 0), (ya, 0)],
        [got[(B, 0, 0)], (yb3, 0), (xb2r, 0), (xb2l, 0)],
    )
    pieces = whole_call(
        split_kernel, [jax.ShapeDtypeStruct((KS, 8, 128), BF)] * 8, "split", keep, send(out, CORE)
    )
    pieces = [pieces[0]] + [
        send(pieces[n], moves(lambda x, y, z, c, n=n: (x + n // 2, y + 2 * (n % 2), z, c))) for n in range(1, 8)
    ]
    pieces = pl.pallas_call(
        turn_kernel,
        out_shape=[jax.ShapeDtypeStruct((16, KS * 8), BF)] * 8,
        scratch_shapes=[pltpu.VMEM((KS * 8, 128), F32)],
        compiler_params=pltpu.CompilerParams(vmem_limit_bytes=VMEM),
        name="turn",
    )(*pieces)
    pieces = [pieces[0]] + [
        send(pieces[n], moves(lambda x, y, z, c, n=n: (x, y ^ (n % 2), z + n // 2, c))) for n in range(1, 8)
    ]
    tensor, diffusion = whole_call(
        finish_kernel,
        [jax.ShapeDtypeStruct((8, 16, 32), F32), jax.ShapeDtypeStruct((4, 8), F32)],
        "finish",
        *pieces,
    )
    return tensor.transpose(2, 0, 1), diffusion


def solution(mesh):
    return jax.shard_map(
        on_device,
        mesh=mesh,
        in_specs=(P("snap", None, "elem"), P("snap", None), P("elem"), P(None, None, "elem"), P()),
        out_specs=(P(None, "snap", "elem"), P("elem", "snap")),
        check_vma=False,
    )
```

```python
import math

import jax
import jax.numpy as jnp
import numpy as np
from jax import lax
from jax.experimental import pallas as pl
from jax.experimental.pallas import tpu as pltpu
from jax.sharding import PartitionSpec as P

GLL = 8
NPE = 512
AXES = ("elem", "snap")
BF = jnp.bfloat16
F32 = jnp.float32


def legendre_pair(value, points):
    before, current = (1.0, value)
    for degree in range(2, points):
        before, current = (
            current,
            ((2 * degree - 1) * value * current - (degree - 1) * before) / degree,
        )
    return (before, current)


def derivative_tables(points):
    degree = points - 1
    nodes = [math.cos(math.pi * index / degree) for index in range(points)]
    for sweep in range(100):
        updated = []
        for value in nodes:
            before, current = legendre_pair(value, points)
            updated.append(value - (value * current - before) / (points * current))
        nodes = updated
    abscissae = sorted(nodes)
    evaluated = [legendre_pair(value, points)[1] for value in abscissae]
    matrix = np.zeros((points, points))
    for first in range(points):
        for second in range(points):
            if first != second:
                matrix[first, second] = evaluated[first] / (
                    evaluated[second] * (abscissae[first] - abscissae[second])
                )
    matrix[0, 0] = -degree * (degree + 1) / 4.0
    matrix[degree, degree] = degree * (degree + 1) / 4.0
    identity = np.eye(points)
    stacked = np.concatenate(
        [
            np.kron(identity, np.kron(identity, matrix.T)),
            np.kron(identity, np.kron(matrix.T, identity)),
            np.kron(matrix.T, np.kron(identity, identity)),
        ],
        axis=1,
    )
    return jnp.asarray(stacked, jnp.float32).astype(jnp.bfloat16)


def place(x, y, z, core):
    return (z * 2 + y % 2) * 16 + (x * 2 + y // 2) * 2 + core


PLACES = [(x, y, z, core) for x in range(4) for y in range(4) for z in range(4) for core in range(2)]


def moves(shift):
    pairs = []
    for x, y, z, core in PLACES:
        nx, ny, nz, ncore = shift(x, y, z, core)
        pairs.append((place(x, y, z, core), place(nx % 4, ny % 4, nz % 4, ncore)))
    return pairs


CORE = moves(lambda x, y, z, c: (x, y, z, 1 - c))
FORWARD = moves(lambda x, y, z, c: (x + 1 - 2 * c, y, z, c))
BACK = moves(lambda x, y, z, c: (x - 1 + 2 * c, y, z, c))
Y2 = moves(lambda x, y, z, c: (x, y + 2, z, c))


def send(value, pairs, name):
    with jax.named_scope(name):
        return lax.ppermute(value, AXES, pairs)


ITEM = (3, 128, NPE)
ITEM_BYTES = 3 * 128 * NPE * 2
MIB = 1024 * 1024
TINY = pl.CostEstimate(flops=1, bytes_accessed=1, transcendentals=0)
TABLE = 16
TOKEN = (8, 128)


def cut(table, fields, wanted, name, coef=None, token=None):
    planes = 6 if coef is None else 7
    count = len(wanted)
    others = [array for array in (coef, token) if array is not None]

    def kernel(table_ref, fields_ref, coef_ref, *refs):
        outs, token_ref, sems = refs[:count], refs[count], refs[count + 1]
        copies = []
        for n, dx in enumerate(wanted):
            lanes = pl.ds(pl.multiple_of(table_ref[12 + dx] * 1024, 1024), 1024)
            for c in range(6):
                copies.append(
                    pltpu.make_async_copy(fields_ref.at[c, :, lanes], outs[n].at[0, c], sems.at[n * 6 + c])
                )
        for copy in copies:
            copy.start()
        token_ref[...] = jnp.zeros(TOKEN, F32)
        if coef is not None:
            outs[0][0, 6, :, :128] = coef_ref[...]
            outs[0][0, 6, :, 128:] = jnp.zeros((128, 896), BF)
        for copy in copies:
            copy.wait()

    return pl.pallas_call(
        kernel,
        grid_spec=pltpu.PrefetchScalarGridSpec(
            num_scalar_prefetch=1,
            grid=(1,),
            in_specs=[
                pl.BlockSpec(memory_space=pl.ANY),
                pl.BlockSpec(memory_space=pl.ANY) if coef is None else whole((128, 128)),
            ],
            out_specs=[whole((1, planes, 128, 1024))] * count + [whole(TOKEN)],
            scratch_shapes=[pltpu.SemaphoreType.DMA((6 * count,))],
        ),
        out_shape=[bf16(1, planes, 128, 1024)] * count + [jax.ShapeDtypeStruct(TOKEN, F32)],
        compiler_params=pltpu.CompilerParams(vmem_limit_bytes=16 * MIB),
        cost_estimate=TINY,
        name=name,
    )(table, fields, *others)


def own_spec(half, dx, dy):
    return pl.BlockSpec(ITEM, lambda i, table, *rest: (half, 0, table[dx * 2 + dy]))


def other_spec(half, dy):
    return pl.BlockSpec((1,) + ITEM, lambda i, table, *rest: (0, half, 0, table[8 + dy]))


def row_spec(array, row):
    return pl.BlockSpec((1,) + array.shape[1:], lambda i, *rest: (row, 0, 0, 0))


def whole(shape):
    return pl.BlockSpec(shape, lambda i, *rest: (0,) * len(shape))


def pin_kernel(*refs):
    refs[-1][...] = jnp.zeros(TOKEN, F32)


def pin(*arrays):
    return pl.pallas_call(
        pin_kernel,
        in_specs=[pl.BlockSpec(memory_space=pl.ANY)] * len(arrays),
        out_specs=pl.BlockSpec(memory_space=pltpu.VMEM),
        out_shape=jax.ShapeDtypeStruct(TOKEN, F32),
        compiler_params=pltpu.CompilerParams(vmem_limit_bytes=4 * MIB),
        cost_estimate=TINY,
        name="pin",
    )(*arrays)


def project(coef, own, other, c):
    rows = jnp.concatenate([own[c], other[0, c]], axis=0)
    return jnp.dot(coef, rows, preferred_element_type=F32)


def sums(shared, items, outs, name, before=(), coefs=None):
    table, fields, coef, chunks = shared
    operands, specs, plan = [], [], []
    for (half, dx, dy), adds in items:
        entry = []
        for array, spec in [(fields, own_spec(half, dx, dy)), (chunks[dx], other_spec(half, dy))] + [
            (array, row_spec(array, row)) for array, row in adds
        ]:
            entry.append(len(operands))
            operands.append(array)
            specs.append(spec)
        plan.append(entry)
    if coefs is None:
        first, first_specs = [coef], [whole((128, 256))]
    else:
        first = list(coefs)
        first_specs = [whole((128, 128)), pl.BlockSpec((1, 1, 128, 128), lambda i, table: (0, 6, 0, 0))]

    def kernel(table_ref, *refs):
        refs = refs[len(before) :]
        if coefs is None:
            rows = refs[0][...]
        else:
            rows = jnp.concatenate([refs[0][...].T, refs[1][0, 0].T], axis=1)
        refs = refs[len(first) :]
        ins, results = refs[: len(operands)], refs[len(operands) :]
        results[len(outs)][...] = jnp.zeros(TOKEN, F32)
        if coefs is not None:
            results[-1][...] = rows
        for number, group in enumerate(outs):
            for position, item in enumerate(group):
                own, other, *adds = plan[item]
                for c in range(3):
                    total = project(rows, ins[own], ins[other], c)
                    for add in adds:
                        total = total + ins[add][0, c].astype(F32)
                    results[number][position, c] = total.astype(BF)

    shapes = [bf16(len(group), *ITEM) for group in outs] + [jax.ShapeDtypeStruct(TOKEN, F32)]
    if coefs is not None:
        shapes.append(bf16(128, 256))
    return pl.pallas_call(
        kernel,
        grid_spec=pltpu.PrefetchScalarGridSpec(
            num_scalar_prefetch=1,
            grid=(1,),
            in_specs=[pl.BlockSpec(memory_space=pl.ANY)] * len(before) + first_specs + specs,
            out_specs=[whole(shape.shape) for shape in shapes],
        ),
        out_shape=shapes,
        compiler_params=pltpu.CompilerParams(vmem_limit_bytes=16 * MIB),
        cost_estimate=TINY,
        name=name,
    )(table, *before, *first, *operands)


KG = 8
BLOCKS = 32 // KG + 1


def assemble_kernel(counts, table, out_modes, token, coef_ref, tables_ref, weight_ref, metric_ref, *refs):
    fields_u, refs = refs[:2], refs[2:]
    fields_b, refs = refs[:2], refs[2:]
    adds_u, refs = refs[: counts[0]], refs[counts[0] :]
    adds_b, refs = refs[: counts[1]], refs[counts[1] :]
    out_ref, zt_ref, z_ref, g_ref, cb_ref, pick_k, pick_d = refs
    half_weight = 0.5 * weight_ref[...]

    columns = lax.broadcasted_iota(jnp.int32, (16, 128), 1)
    pick_d[...] = jnp.zeros((128, 128), F32)
    for k in range(32):
        hot = (columns == out_modes[k]).astype(F32)
        pick_k[k * 16 : k * 16 + 16, :] = hot.astype(BF)
        row = (k // 4) * 16 + k % 4
        pick_d[row : row + 1, :] = hot[:1]
    chosen_d = pick_d[...].astype(BF)

    coef = coef_ref[...]
    for a in range(3):
        u = project(coef, *fields_u, a)
        for ref in adds_u:
            u = u + ref[0, a].astype(F32)
        b = project(coef, *fields_b, a)
        for ref in adds_b:
            b = b + ref[0, a].astype(F32)
        for sign, z in ((0, u + b), (1, u - b)):
            zt_ref[1 - sign, a] = z.T.astype(BF)
            z = z.astype(BF)
            z_ref[sign, a * 128 : a * 128 + 128] = z
            cb_ref[sign, a] = (
                jnp.dot(pick_k[...], z, preferred_element_type=F32) * half_weight
            ).astype(BF)

    diffusion = None
    for sign in range(2):
        derived = jnp.dot(z_ref[sign], tables_ref[...], preferred_element_type=F32)
        for a in range(3):
            part = derived[a * 128 : a * 128 + 128]
            for b in range(3):
                grad = metric_ref[0, b : b + 1, :] * part[:, :NPE]
                grad = grad + metric_ref[1, b : b + 1, :] * part[:, NPE : 2 * NPE]
                grad = grad + metric_ref[2, b : b + 1, :] * part[:, 2 * NPE :]
                grad = grad.astype(BF)
                g_ref[sign, a, b] = grad
                picked = jnp.dot(chosen_d, grad, preferred_element_type=F32) * half_weight
                term = lax.dot_general(
                    grad, picked.astype(BF), (((1,), (1,)), ((), ())), preferred_element_type=F32
                )
                diffusion = term if diffusion is None else diffusion + term
    diffusion = diffusion.astype(BF).reshape(16, 8, 128)
    for elem in range(8):
        out_ref[elem, :, BLOCKS - 1] = diffusion
    group = lax.broadcasted_iota(jnp.int32, (128, 128), 1) // 16

    def rows_of(step, carry):
        total = None
        for sign in range(2):
            for b in range(3):
                pieces = []
                for t in range(KG):
                    start = pl.multiple_of((step * KG + t) * 16, 16)
                    product = None
                    for a in range(3):
                        picked = cb_ref[sign, a, pl.ds(start, 16), :][None]
                        term = g_ref[sign, a, b].reshape(8, 16, NPE) * picked
                        product = term if product is None else product + term
                    pieces.append(product.reshape(128, NPE))
                term = jnp.dot(jnp.concatenate(pieces, axis=0), zt_ref[sign, b], preferred_element_type=F32)
                total = term if total is None else total + term
        turned = [total[:128]] + [
            pltpu.roll(total[t * 128 : t * 128 + 128], 16 * t, 1) for t in range(1, KG)
        ]
        for elem in range(8):
            block = turned[0]
            for t in range(1, KG):
                block = jnp.where(group == (elem + t) % 8, turned[t], block)
            out_ref[elem, :, pl.ds(step, 1)] = block.astype(BF).reshape(16, 1, 8, 128)
        return carry

    lax.fori_loop(0, 32 // KG, rows_of, 0)


def assemble(shared, out_modes, tables, weights, metric, adds_u, adds_b, token):
    table, fields, coef, chunks = shared

    def kernel(*args):
        assemble_kernel((len(adds_u), len(adds_b)), *args)

    adds = adds_u + adds_b
    shape = (8, 16, BLOCKS, 8, 128)
    return pl.pallas_call(
        kernel,
        grid_spec=pltpu.PrefetchScalarGridSpec(
            num_scalar_prefetch=2,
            grid=(1,),
            in_specs=[
                pl.BlockSpec(memory_space=pl.ANY),
                whole((128, 256)),
                whole(tables.shape),
                pl.BlockSpec((1, NPE), lambda i, table, chosen: (0, table[0])),
                pl.BlockSpec((3, 3, NPE), lambda i, table, chosen: (0, 0, table[0])),
                own_spec(0, 0, 0),
                other_spec(0, 0),
                own_spec(1, 0, 0),
                other_spec(1, 0),
            ]
            + [row_spec(array, row) for array, row in adds],
            out_specs=whole(shape),
            scratch_shapes=[
                pltpu.VMEM((2, 3, NPE, 128), BF),
                pltpu.VMEM((2, 384, NPE), BF),
                pltpu.VMEM((2, 3, 3, 128, NPE), BF),
                pltpu.VMEM((2, 3, 512, NPE), BF),
                pltpu.VMEM((512, 128), BF),
                pltpu.VMEM((128, 128), F32),
            ],
        ),
        out_shape=jax.ShapeDtypeStruct(shape, BF),
        compiler_params=pltpu.CompilerParams(vmem_limit_bytes=32 * MIB),
        cost_estimate=TINY,
        name="assemble",
    )(table, out_modes, token, coef, tables, weights, metric, fields, chunks[0], fields, chunks[0],
      *[array for array, row in adds])


def finish_kernel(table, in_ref, tensor_ref, diffusion_ref):
    total = jnp.sum(in_ref[...].astype(F32), axis=0).reshape(BLOCKS * 8, 128)
    total = jnp.concatenate([total, jnp.zeros((128 - BLOCKS * 8, 128), F32)], axis=0)
    shift = lax.rem(128 - 16 * table[10], 128)
    turned = pltpu.roll(total, shift, 1).T
    lane = lax.broadcasted_iota(jnp.int32, (16, 128), 1) % 8
    for j in range(8):
        rows = None
        for t in range(8):
            part = turned[t * 16 : t * 16 + 16]
            if t != j:
                part = pltpu.roll(part, (t - j) % 128, 1)
            rows = part if rows is None else jnp.where(lane == t, part, rows)
        tensor_ref[j] = rows[:, :32]
    diffusion_ref[...] = turned[:4, 32:40]


def finish(table, shares):
    return pl.pallas_call(
        finish_kernel,
        grid_spec=pltpu.PrefetchScalarGridSpec(
            num_scalar_prefetch=1,
            grid=(1,),
            in_specs=[whole(shares.shape)],
            out_specs=[whole((8, 16, 32)), whole((4, 8))],
        ),
        out_shape=[jax.ShapeDtypeStruct((8, 16, 32), F32), jax.ShapeDtypeStruct((4, 8), F32)],
        compiler_params=pltpu.CompilerParams(vmem_limit_bytes=12 * MIB),
        name="finish",
    )(table, shares)


def bf16(*shape):
    return jax.ShapeDtypeStruct(shape, BF)


def on_device(snapshots, coefficients, mass_weights, metric, out_modes):
    fields = snapshots.transpose(1, 0, 2)
    snap, elem = lax.axis_index("snap"), lax.axis_index("elem")
    x, y_hi, core = snap // 4, (snap // 2) % 2, snap % 2
    slot = lax.iota(jnp.int32, TABLE)
    table = core * 8 + ((x + (slot // 2) * (1 + 2 * core)) % 4) * 2 + (y_hi ^ (slot % 2))
    table = jnp.where(slot < 8, table, jnp.where(slot < 10, y_hi ^ (slot % 2), elem))
    table = jnp.where(slot < 12, table, (1 - core) * 4 + (x + slot * (3 - 2 * core)) % 4).astype(jnp.int32)

    near, token = cut(table, fields, [2], "cut_near", coef=coefficients)
    *rest, token = cut(table, fields, [1, 3, 0], "cut_far", token=token)
    near = send(near, CORE, "near")
    chunks = {2: near}
    for dx, chunk in zip((1, 3, 0), rest):
        chunks[dx] = send(chunk, CORE, "far")

    U, B = 0, 1
    rows = None

    def total(items, outs, name, *before):
        nonlocal token, rows
        shared = (table, fields, rows, chunks)
        if rows is None:
            result = sums(shared, items, outs, name, (token,) + before, (coefficients, near))
            rows = result[-1]
        else:
            result = sums(shared, items, outs, name, (token,) + before)
        token = result[len(outs)]
        return result[: len(outs)]

    yb1, xa1 = total([((B, 2, 1), []), ((U, 2, 0), []), ((U, 2, 1), [])], [[0], [1, 2]], "first")
    yb1, xa1 = send(yb1, Y2, "yb1"), send(xa1, FORWARD, "xa1")
    yb2, xa2 = total(
        [((B, 1, 1), []), ((B, 3, 1), []), ((U, 3, 0), []), ((U, 3, 1), [])], [[0, 1], [2, 3]], "second"
    )
    yb2, xa2 = send(yb2, Y2, "yb2"), send(xa2, BACK, "xa2")
    xa3, xb1, yb3 = total(
        [((U, 1, 0), [(xa1, 0)]), ((U, 1, 1), [(xa1, 1)]), ((B, 2, 0), [(yb1, 0)]), ((B, 0, 1), [])],
        [[0, 1], [2], [3]], "third",
    )
    xa3, xb1, yb3 = send(xa3, FORWARD, "xa3"), send(xb1, FORWARD, "xb1"), send(yb3, Y2, "yb3")
    token = pin(token, xa2, yb2)
    (ya,) = total([((U, 0, 1), [(xa2, 1), (xa3, 1)])], [[0]], "fourth")
    ya = send(ya, Y2, "ya")
    xb3, xb2 = total([((B, 1, 0), [(yb2, 0), (xb1, 0)]), ((B, 3, 0), [(yb2, 1)])], [[0], [1]], "fifth")
    xb3, xb2 = send(xb3, FORWARD, "xb3"), send(xb2, BACK, "xb2")

    token = pin(token, ya)

    shares = assemble(
        (table, fields, rows, chunks), out_modes, derivative_tables(GLL), mass_weights.reshape(1, -1), metric,
        [(xa2, 0), (xa3, 0), (ya, 0)],
        [(yb3, 0), (xb2, 0), (xb3, 0)],
        token,
    )
    shares = lax.all_to_all(shares.reshape(128, BLOCKS, 8, 128), AXES, 0, 0, tiled=True)
    tensor, diffusion = finish(table, shares)
    return tensor.transpose(2, 0, 1), diffusion


def solution(mesh):
    return jax.shard_map(
        on_device,
        mesh=mesh,
        in_specs=(P("snap", None, "elem"), P("snap", None), P("elem"), P(None, None, "elem"), P()),
        out_specs=(P(None, "snap", "elem"), P("elem", "snap")),
        check_vma=False,
    )
```

```python
import math

import jax
import jax.numpy as jnp
import numpy as np
from jax import lax
from jax.experimental import pallas as pl
from jax.experimental.pallas import tpu as pltpu
from jax.sharding import PartitionSpec as P

GLL = 8
NPE = 512
AXES = ("elem", "snap")
BF = jnp.bfloat16
F32 = jnp.float32


def legendre_pair(value, points):
    before, current = (1.0, value)
    for degree in range(2, points):
        before, current = (
            current,
            ((2 * degree - 1) * value * current - (degree - 1) * before) / degree,
        )
    return (before, current)


def derivative_tables(points):
    degree = points - 1
    nodes = [math.cos(math.pi * index / degree) for index in range(points)]
    for sweep in range(100):
        updated = []
        for value in nodes:
            before, current = legendre_pair(value, points)
            updated.append(value - (value * current - before) / (points * current))
        nodes = updated
    abscissae = sorted(nodes)
    evaluated = [legendre_pair(value, points)[1] for value in abscissae]
    matrix = np.zeros((points, points))
    for first in range(points):
        for second in range(points):
            if first != second:
                matrix[first, second] = evaluated[first] / (
                    evaluated[second] * (abscissae[first] - abscissae[second])
                )
    matrix[0, 0] = -degree * (degree + 1) / 4.0
    matrix[degree, degree] = degree * (degree + 1) / 4.0
    identity = np.eye(points)
    stacked = np.concatenate(
        [
            np.kron(identity, np.kron(identity, matrix.T)),
            np.kron(identity, np.kron(matrix.T, identity)),
            np.kron(matrix.T, np.kron(identity, identity)),
        ],
        axis=1,
    )
    return jnp.asarray(stacked, jnp.float32).astype(jnp.bfloat16)


def place(x, y, z, core):
    return (z * 2 + y % 2) * 16 + (x * 2 + y // 2) * 2 + core


PLACES = [(x, y, z, core) for x in range(4) for y in range(4) for z in range(4) for core in range(2)]


def moves(shift):
    pairs = []
    for x, y, z, core in PLACES:
        nx, ny, nz, ncore = shift(x, y, z, core)
        pairs.append((place(x, y, z, core), place(nx % 4, ny % 4, nz % 4, ncore)))
    return pairs


CORE = moves(lambda x, y, z, c: (x, y, z, 1 - c))
FORWARD = moves(lambda x, y, z, c: (x + 1 - 2 * c, y, z, c))
BACK = moves(lambda x, y, z, c: (x - 1 + 2 * c, y, z, c))
Y2 = moves(lambda x, y, z, c: (x, y + 2, z, c))


def lines(key):
    groups = {}
    for where in PLACES:
        groups.setdefault(key(*where), []).append(place(*where))
    return [sorted(group) for group in groups.values()]


SAME_CORE = lines(lambda x, y, z, c: c)


def send(value, pairs, name):
    with jax.named_scope(name):
        return lax.ppermute(value, AXES, pairs)


ITEM = (3, 128, NPE)
ITEM_BYTES = 3 * 128 * NPE * 2
MIB = 1024 * 1024
TINY = pl.CostEstimate(flops=1, bytes_accessed=1, transcendentals=0)
TABLE = 18
TOKEN = (8, 128)


def cut(table, fields, groups, name, space, token, coef=None):
    extra = 0 if coef is None else 1
    count = len(groups)
    total = sum(len(group) for group in groups)

    def kernel(table_ref, fields_ref, token_in, *refs):
        outs, token_ref, sems = refs[extra : extra + count], refs[-2], refs[-1]
        copies = []
        if coef is not None:
            copies.append(
                pltpu.make_async_copy(
                    refs[0], outs[0].at[3 * total, :, pl.ds(0, 128)], sems.at[total]
                )
            )
        slot = 0
        for number, group in enumerate(groups):
            for n, (half, dx, dy) in enumerate(group):
                lanes = pl.ds(pl.multiple_of(table_ref[8 + dx * 2 + dy] * NPE, NPE), NPE)
                copies.append(
                    pltpu.make_async_copy(
                        fields_ref.at[pl.ds(half * 3, 3), :, lanes],
                        outs[number].at[pl.ds(3 * n, 3)],
                        sems.at[slot],
                    )
                )
                slot += 1
        for copy in copies:
            copy.start()
        token_ref[...] = jnp.zeros(TOKEN, F32)
        if coef is not None:
            outs[0][3 * total, :, 128:] = jnp.zeros((128, NPE - 128), BF)
        for copy in copies:
            copy.wait()

    anywhere = pl.BlockSpec(memory_space=pl.ANY)
    others = [token] if coef is None else [token, coef]
    shapes = [bf16(3 * len(group) + extra, 128, NPE) for group in groups]
    return pl.pallas_call(
        kernel,
        grid_spec=pltpu.PrefetchScalarGridSpec(
            num_scalar_prefetch=1,
            grid=(1,),
            in_specs=[pl.BlockSpec(memory_space=space)] + [anywhere] * len(others),
            out_specs=[whole(shape.shape) for shape in shapes] + [whole(TOKEN)],
            scratch_shapes=[pltpu.SemaphoreType.DMA((total + 1,))],
        ),
        out_shape=shapes + [jax.ShapeDtypeStruct(TOKEN, F32)],
        compiler_params=pltpu.CompilerParams(vmem_limit_bytes=16 * MIB),
        cost_estimate=TINY,
        name=name,
    )(table, fields, *others)


def own_spec(half, dx, dy):
    return pl.BlockSpec(ITEM, lambda i, table, *rest: (half, 0, table[dx * 2 + dy]))


def other_spec(row):
    return pl.BlockSpec(ITEM, lambda i, *rest: (row, 0, 0))


def row_spec(row):
    return pl.BlockSpec((1,) + ITEM, lambda i, *rest: (row, 0, 0, 0))


def whole(shape):
    return pl.BlockSpec(shape, lambda i, *rest: (0,) * len(shape))


def pin_kernel(*refs):
    refs[-1][...] = jnp.zeros(TOKEN, F32)


def pin(*arrays):
    return pl.pallas_call(
        pin_kernel,
        in_specs=[pl.BlockSpec(memory_space=pl.ANY)] * len(arrays),
        out_specs=pl.BlockSpec(memory_space=pltpu.VMEM),
        out_shape=jax.ShapeDtypeStruct(TOKEN, F32),
        compiler_params=pltpu.CompilerParams(vmem_limit_bytes=4 * MIB),
        cost_estimate=TINY,
        name="pin",
    )(*arrays)


def project(coef, own, other, c):
    rows = jnp.concatenate([own[c], other[c]], axis=0)
    return jnp.dot(coef, rows, preferred_element_type=F32)


def sums(shared, items, outs, name, before=(), coefs=None):
    table, fields, coef, chunks = shared
    operands, specs, plan = [], [], []
    for (half, dx, dy), adds in items:
        entry = []
        other, row = chunks[(half, dx, dy)]
        for array, spec in [(fields, own_spec(half, dx, dy)), (other, other_spec(row))] + [
            (array, row_spec(row)) for array, row in adds
        ]:
            entry.append(len(operands))
            operands.append(array)
            specs.append(spec)
        plan.append(entry)
    if coefs is None:
        first, first_specs = [coef], [whole((128, 256))]
    else:
        first = list(coefs)
        first_specs = [whole((128, 128)), pl.BlockSpec((1, 128, 128), lambda i, table: (9, 0, 0))]

    def kernel(table_ref, *refs):
        refs = refs[len(before) :]
        if coefs is None:
            rows = refs[0][...]
        else:
            rows = jnp.concatenate([refs[0][...], refs[1][0]], axis=1)
        refs = refs[len(first) :]
        ins, results = refs[: len(operands)], refs[len(operands) :]
        results[len(outs)][...] = jnp.zeros(TOKEN, F32)
        if coefs is not None:
            results[-1][...] = rows
        for number, group in enumerate(outs):
            for position, item in enumerate(group):
                own, other, *adds = plan[item]
                for c in range(3):
                    total = project(rows, ins[own], ins[other], c)
                    for add in adds:
                        total = total + ins[add][0, c].astype(F32)
                    results[number][position, c] = total.astype(BF)

    shapes = [bf16(len(group), *ITEM) for group in outs] + [jax.ShapeDtypeStruct(TOKEN, F32)]
    if coefs is not None:
        shapes.append(bf16(128, 256))
    return pl.pallas_call(
        kernel,
        grid_spec=pltpu.PrefetchScalarGridSpec(
            num_scalar_prefetch=1,
            grid=(1,),
            in_specs=[pl.BlockSpec(memory_space=pl.ANY)] * len(before) + first_specs + specs,
            out_specs=[whole(shape.shape) for shape in shapes],
        ),
        out_shape=shapes,
        compiler_params=pltpu.CompilerParams(vmem_limit_bytes=16 * MIB),
        cost_estimate=TINY,
        name=name,
    )(table, *before, *first, *operands)


KG = 8
BLOCKS = 32 // KG + 1


def assemble_kernel(counts, table, out_modes, token, coef_ref, tables_ref, weight_ref, metric_ref, *refs):
    fields_u, refs = refs[:2], refs[2:]
    fields_b, refs = refs[:2], refs[2:]
    adds_u, refs = refs[: counts[0]], refs[counts[0] :]
    adds_b, refs = refs[: counts[1]], refs[counts[1] :]
    keep_ref, send_ref, z_ref, g_ref, cb_ref, pick_k, pick_d = refs
    first = table[17] == 0

    def put(elem, step, block):
        sides = block.reshape(8, 2, 8, 128)
        keep_ref[elem, :, step] = jnp.where(first, sides[:, 0], sides[:, 1]).astype(BF)
        send_ref[elem, :, step] = jnp.where(first, sides[:, 1], sides[:, 0]).astype(BF)

    half_weight = 0.5 * weight_ref[...]

    columns = lax.broadcasted_iota(jnp.int32, (1, 128), 1)
    pick_d[...] = jnp.zeros((128, 128), F32)
    for k in range(32):
        hot = (columns == out_modes[k]).astype(F32)
        pick_k[k : k + 1, :] = hot
        row = (k // 4) * 16 + k % 4
        pick_d[row : row + 1, :] = hot
    chosen = pick_k[...].astype(BF)

    coef = coef_ref[...]
    for a in range(3):
        u = project(coef, *fields_u, a)
        for ref in adds_u:
            u = u + ref[0, a].astype(F32)
        b = project(coef, *fields_b, a)
        for ref in adds_b:
            b = b + ref[0, a].astype(F32)
        for sign, z in ((0, u + b), (1, u - b)):
            z = z.astype(BF)
            z_ref[sign, a * 128 : a * 128 + 128] = z
            picked = jnp.dot(chosen, z, preferred_element_type=F32) * half_weight
            for k in range(32):
                cb_ref[sign, a, k * 16 : k * 16 + 16, :] = jnp.broadcast_to(
                    picked[k : k + 1], (16, NPE)
                ).astype(BF)

    half = NPE // 2
    gram = None
    for sign in range(2):
        z = z_ref[sign]
        derived = []
        for r in range(2):
            block = tables_ref[:half, r * NPE : r * NPE + half]
            derived.append([
                jnp.dot(z[:, side * half : side * half + half], block, preferred_element_type=F32)
                for side in range(2)
            ])
        full = jnp.dot(z, tables_ref[:, 2 * NPE :], preferred_element_type=F32)
        derived.append([full[:, :half], full[:, half:]])
        for a in range(3):
            for b in range(3):
                sides = []
                for side in range(2):
                    lanes = slice(side * half, side * half + half)
                    grad = None
                    for r in range(3):
                        term = metric_ref[r, b : b + 1, lanes] * derived[r][side][a * 128 : a * 128 + 128]
                        grad = term if grad is None else grad + term
                    sides.append(grad)
                grad = jnp.concatenate(sides, axis=1).astype(BF)
                g_ref[sign, a, b] = grad
                weighted = (grad.astype(F32) * half_weight).astype(BF)
                term = lax.dot_general(
                    grad, weighted, (((1,), (1,)), ((), ())), preferred_element_type=F32
                )
                gram = term if gram is None else gram + term
    diffusion = lax.dot_general(
        gram.astype(BF), pick_d[...].astype(BF), (((1,), (1,)), ((), ())), preferred_element_type=F32
    )
    for elem in range(8):
        put(elem, BLOCKS - 1, diffusion)
    group = lax.broadcasted_iota(jnp.int32, (128, 128), 1) // 16

    def rows_of(step):
        total = None
        for sign in range(2):
            for b in range(3):
                pieces = []
                for t in range(KG):
                    start = (step * KG + t) * 16
                    product = None
                    for a in range(3):
                        picked = cb_ref[sign, a, pl.ds(start, 16), :][None]
                        term = g_ref[sign, a, b].reshape(8, 16, NPE) * picked
                        product = term if product is None else product + term
                    pieces.append(product.reshape(128, NPE))
                modes = z_ref[1 - sign, b * 128 : b * 128 + 128]
                term = lax.dot_general(
                    jnp.concatenate(pieces, axis=0), modes, (((1,), (1,)), ((), ())), preferred_element_type=F32
                )
                total = term if total is None else total + term
        turned = [total[:128]] + [
            pltpu.roll(total[t * 128 : t * 128 + 128], 16 * t, 1) for t in range(1, KG)
        ]
        for elem in range(8):
            block = turned[0]
            for t in range(1, KG):
                block = jnp.where(group == (elem + t) % 8, turned[t], block)
            put(elem, step, block)

    for step in range(32 // KG):
        rows_of(step)


def assemble(shared, out_modes, tables, weights, metric, adds_u, adds_b, token):
    table, fields, coef, chunks = shared

    def kernel(*args):
        assemble_kernel((len(adds_u), len(adds_b)), *args)

    adds = adds_u + adds_b
    out = bf16(8, 8, BLOCKS, 8, 128)
    return pl.pallas_call(
        kernel,
        grid_spec=pltpu.PrefetchScalarGridSpec(
            num_scalar_prefetch=2,
            grid=(1,),
            in_specs=[
                pl.BlockSpec(memory_space=pl.ANY),
                whole((128, 256)),
                whole(tables.shape),
                pl.BlockSpec((1, NPE), lambda i, table, chosen: (0, table[0])),
                pl.BlockSpec((3, 3, NPE), lambda i, table, chosen: (0, 0, table[0])),
                own_spec(0, 0, 0),
                other_spec(chunks[(0, 0, 0)][1]),
                own_spec(1, 0, 0),
                other_spec(chunks[(1, 0, 0)][1]),
            ]
            + [row_spec(row) for array, row in adds],
            out_specs=[whole(out.shape)] * 2,
            scratch_shapes=[
                pltpu.VMEM((2, 384, NPE), BF),
                pltpu.VMEM((2, 3, 3, 128, NPE), BF),
                pltpu.VMEM((2, 3, 512, NPE), BF),
                pltpu.VMEM((32, 128), F32),
                pltpu.VMEM((128, 128), F32),
            ],
        ),
        out_shape=[out] * 2,
        compiler_params=pltpu.CompilerParams(vmem_limit_bytes=32 * MIB),
        cost_estimate=TINY,
        name="assemble",
    )(table, out_modes, token, coef, tables, weights, metric, fields, chunks[(0, 0, 0)][0], fields, chunks[(1, 0, 0)][0],
      *[array for array, row in adds])


def add_kernel(keep_ref, got_ref, out_ref):
    out_ref[...] = (keep_ref[...].astype(F32) + got_ref[...].astype(F32)).astype(BF)


def add(keep, got):
    return pl.pallas_call(
        add_kernel,
        out_shape=bf16(*keep.shape),
        compiler_params=pltpu.CompilerParams(vmem_limit_bytes=12 * MIB),
        name="add",
    )(keep, got)


def finish_kernel(table, in_ref, tensor_ref, diffusion_ref):
    total = jnp.sum(in_ref[...].astype(F32), axis=0).reshape(BLOCKS * 8, 128)
    total = jnp.concatenate([total, jnp.zeros((128 - BLOCKS * 8, 128), F32)], axis=0)
    shift = lax.rem(128 - 16 * table[16], 128)
    turned = pltpu.roll(total, shift, 1).T
    lane = lax.broadcasted_iota(jnp.int32, (16, 128), 1) % 8
    for j in range(8):
        rows = None
        for t in range(8):
            part = turned[t * 16 : t * 16 + 16]
            if t != j:
                part = pltpu.roll(part, (t - j) % 128, 1)
            rows = part if rows is None else jnp.where(lane == t, part, rows)
        tensor_ref[j] = rows[:, :32]
    diffusion_ref[...] = turned[:4, 32:40]


def finish(table, shares):
    return pl.pallas_call(
        finish_kernel,
        grid_spec=pltpu.PrefetchScalarGridSpec(
            num_scalar_prefetch=1,
            grid=(1,),
            in_specs=[whole(shares.shape)],
            out_specs=[whole((8, 16, 32)), whole((4, 8))],
        ),
        out_shape=[jax.ShapeDtypeStruct((8, 16, 32), F32), jax.ShapeDtypeStruct((4, 8), F32)],
        compiler_params=pltpu.CompilerParams(vmem_limit_bytes=12 * MIB),
        name="finish",
    )(table, shares)


def bf16(*shape):
    return jax.ShapeDtypeStruct(shape, BF)


def on_device(snapshots, coefficients, mass_weights, metric, out_modes):
    fields = snapshots.transpose(1, 0, 2)
    coefficients = coefficients.T
    snap, elem = lax.axis_index("snap"), lax.axis_index("elem")
    x, y_hi, core = snap // 4, (snap // 2) % 2, snap % 2
    slot = lax.iota(jnp.int32, TABLE)
    side = jnp.where(slot < 8, core, 1 - core)
    table = side * 8 + ((x + ((slot // 2) % 4) * (1 + 2 * side)) % 4) * 2 + (y_hi ^ (slot % 2))
    table = jnp.where(slot < 16, table, jnp.where(slot < 17, elem, core)).astype(jnp.int32)

    U, B = 0, 1
    chunks, token, rows = {}, jnp.zeros(TOKEN, F32), None

    def trade(groups, name, space, coef=None):
        nonlocal token
        *values, token = cut(table, fields, groups, "cut_" + name, space, token, coef)
        for value, group in zip(values, groups):
            got = send(value, CORE, name)
            for row, key in enumerate(group):
                chunks[key] = (got, row)

    def total(items, outs, name, *before):
        nonlocal token, rows
        coefs = (coefficients, chunks[(B, 2, 1)][0]) if rows is None else None
        result = sums((table, fields, rows, chunks), items, outs, name, (token,) + before, coefs)
        if coefs is not None:
            rows = result[-1]
        token = result[len(outs)]
        return result[: len(outs)]

    trade([[(B, 2, 1), (U, 2, 0), (U, 2, 1)]], "near", pltpu.HBM, coefficients)
    trade(
        [
            [(B, 1, 1), (B, 3, 1), (U, 3, 0), (U, 3, 1)],
            [(B, 2, 0), (B, 0, 1), (U, 1, 0), (U, 1, 1)],
            [(B, 1, 0), (B, 3, 0), (U, 0, 1), (U, 0, 0), (B, 0, 0)],
        ],
        "far", pl.ANY,
    )
    yb1, xa1 = total([((B, 2, 1), []), ((U, 2, 0), []), ((U, 2, 1), [])], [[0], [1, 2]], "first")
    yb1, xa1 = send(yb1, Y2, "yb1"), send(xa1, FORWARD, "xa1")
    yb2, xa2 = total(
        [((B, 1, 1), []), ((B, 3, 1), []), ((U, 3, 0), []), ((U, 3, 1), [])], [[0, 1], [2, 3]], "second"
    )
    yb2, xa2 = send(yb2, Y2, "yb2"), send(xa2, BACK, "xa2")
    xb1, xa3, yb3 = total(
        [((B, 2, 0), [(yb1, 0)]), ((U, 1, 0), [(xa1, 0)]), ((U, 1, 1), [(xa1, 1)]), ((B, 0, 1), [])],
        [[0], [1, 2], [3]], "third",
    )
    xb1, xa3, yb3 = send(xb1, FORWARD, "xb1"), send(xa3, FORWARD, "xa3"), send(yb3, Y2, "yb3")
    token = pin(token, xa2, yb2)
    (ya,) = total([((U, 0, 1), [(xa2, 1), (xa3, 1)])], [[0]], "fourth")
    ya = send(ya, Y2, "ya")
    xb3, xb2 = total([((B, 1, 0), [(yb2, 0), (xb1, 0)]), ((B, 3, 0), [(yb2, 1)])], [[0], [1]], "fifth")
    xb3, xb2 = send(xb3, FORWARD, "xb3"), send(xb2, BACK, "xb2")
    token = pin(token, ya)

    keep, shares = assemble(
        (table, fields, rows, chunks), out_modes, derivative_tables(GLL), mass_weights.reshape(1, -1), metric,
        [(xa2, 0), (xa3, 0), (ya, 0)],
        [(yb3, 0), (xb2, 0), (xb3, 0)],
        token,
    )
    shares = add(keep, send(shares, CORE, "shares")).reshape(64, BLOCKS, 8, 128)
    shares = lax.all_to_all(shares, AXES, 0, 0, axis_index_groups=SAME_CORE, tiled=True)
    tensor, diffusion = finish(table, shares)
    return tensor.transpose(2, 0, 1), diffusion


def solution(mesh):
    return jax.shard_map(
        on_device,
        mesh=mesh,
        in_specs=(P("snap", None, "elem"), P("snap", None), P("elem"), P(None, None, "elem"), P()),
        out_specs=(P(None, "snap", "elem"), P("elem", "snap")),
        check_vma=False,
    )
```

```python
import math

import jax
import jax.numpy as jnp
import numpy as np
from jax import lax
from jax.experimental import pallas as pl
from jax.experimental.pallas import tpu as pltpu
from jax.sharding import PartitionSpec as P

GLL = 8
NPE = 512
AXES = ("elem", "snap")
BF = jnp.bfloat16
F32 = jnp.float32


def legendre_pair(value, points):
    before, current = (1.0, value)
    for degree in range(2, points):
        before, current = (
            current,
            ((2 * degree - 1) * value * current - (degree - 1) * before) / degree,
        )
    return (before, current)


def derivative_tables(points):
    degree = points - 1
    nodes = [math.cos(math.pi * index / degree) for index in range(points)]
    for sweep in range(100):
        updated = []
        for value in nodes:
            before, current = legendre_pair(value, points)
            updated.append(value - (value * current - before) / (points * current))
        nodes = updated
    abscissae = sorted(nodes)
    evaluated = [legendre_pair(value, points)[1] for value in abscissae]
    matrix = np.zeros((points, points))
    for first in range(points):
        for second in range(points):
            if first != second:
                matrix[first, second] = evaluated[first] / (
                    evaluated[second] * (abscissae[first] - abscissae[second])
                )
    matrix[0, 0] = -degree * (degree + 1) / 4.0
    matrix[degree, degree] = degree * (degree + 1) / 4.0
    identity = np.eye(points)
    stacked = np.concatenate(
        [
            np.kron(identity, np.kron(identity, matrix.T)),
            np.kron(identity, np.kron(matrix.T, identity)),
            np.kron(matrix.T, np.kron(identity, identity)),
        ],
        axis=1,
    )
    return jnp.asarray(stacked, jnp.float32).astype(jnp.bfloat16)


def place(x, y, z, core):
    return (z * 2 + y % 2) * 16 + (x * 2 + y // 2) * 2 + core


PLACES = [(x, y, z, core) for x in range(4) for y in range(4) for z in range(4) for core in range(2)]


def moves(shift):
    pairs = []
    for x, y, z, core in PLACES:
        nx, ny, nz, ncore = shift(x, y, z, core)
        pairs.append((place(x, y, z, core), place(nx % 4, ny % 4, nz % 4, ncore)))
    return pairs


CORE = moves(lambda x, y, z, c: (x, y, z, 1 - c))
FORWARD = moves(lambda x, y, z, c: (x + 1 - 2 * c, y, z, c))
BACK = moves(lambda x, y, z, c: (x - 1 + 2 * c, y, z, c))
Y2 = moves(lambda x, y, z, c: (x, y + 2, z, c))


def lines(key):
    groups = {}
    for where in PLACES:
        groups.setdefault(key(*where), []).append(place(*where))
    return [sorted(group) for group in groups.values()]


SAME_CORE = lines(lambda x, y, z, c: c)


def send(value, pairs, name):
    with jax.named_scope(name):
        return lax.ppermute(value, AXES, pairs)


ITEM = (3, 128, NPE)
ITEM_BYTES = 3 * 128 * NPE * 2
MIB = 1024 * 1024
INSIDE = pl.BlockSpec(memory_space=pltpu.VMEM)
TINY = pl.CostEstimate(flops=1, bytes_accessed=1, transcendentals=0)
TABLE = 18
TOKEN = (8, 128)


def cut(table, fields, groups, name, space, token, coef=None):
    extra = 0 if coef is None else 1
    count = len(groups)
    total = sum(len(group) for group in groups)

    def kernel(table_ref, fields_ref, token_in, *refs):
        outs, token_ref, sems = refs[extra : extra + count], refs[-2], refs[-1]
        copies = []
        if coef is not None:
            copies.append(
                pltpu.make_async_copy(
                    refs[0], outs[0].at[3 * total, :, pl.ds(0, 128)], sems.at[total]
                )
            )
        slot = 0
        for number, group in enumerate(groups):
            for n, (half, dx, dy) in enumerate(group):
                lanes = pl.ds(pl.multiple_of(table_ref[8 + dx * 2 + dy] * NPE, NPE), NPE)
                copies.append(
                    pltpu.make_async_copy(
                        fields_ref.at[pl.ds(half * 3, 3), :, lanes],
                        outs[number].at[pl.ds(3 * n, 3)],
                        sems.at[slot],
                    )
                )
                slot += 1
        for copy in copies:
            copy.start()
        token_ref[...] = jnp.zeros(TOKEN, F32)
        if coef is not None:
            outs[0][3 * total, :, 128:] = jnp.zeros((128, NPE - 128), BF)
        for copy in copies:
            copy.wait()

    anywhere = pl.BlockSpec(memory_space=pl.ANY)
    others = [token] if coef is None else [token, coef]
    shapes = [bf16(3 * len(group) + extra, 128, NPE) for group in groups]
    return pl.pallas_call(
        kernel,
        grid_spec=pltpu.PrefetchScalarGridSpec(
            num_scalar_prefetch=1,
            grid=(1,),
            in_specs=[pl.BlockSpec(memory_space=space)] + [anywhere] * len(others),
            out_specs=[whole(shape.shape) for shape in shapes] + [whole(TOKEN)],
            scratch_shapes=[pltpu.SemaphoreType.DMA((total + 1,))],
        ),
        out_shape=shapes + [jax.ShapeDtypeStruct(TOKEN, F32)],
        compiler_params=pltpu.CompilerParams(vmem_limit_bytes=16 * MIB),
        cost_estimate=TINY,
        name=name,
    )(table, fields, *others)


def whole(shape):
    return pl.BlockSpec(shape, lambda i, *rest: (0,) * len(shape))


def pin_kernel(*refs):
    refs[-1][...] = jnp.zeros(TOKEN, F32)


def pin(*arrays):
    return pl.pallas_call(
        pin_kernel,
        in_specs=[pl.BlockSpec(memory_space=pl.ANY)] * len(arrays),
        out_specs=pl.BlockSpec(memory_space=pltpu.VMEM),
        out_shape=jax.ShapeDtypeStruct(TOKEN, F32),
        compiler_params=pltpu.CompilerParams(vmem_limit_bytes=4 * MIB),
        cost_estimate=TINY,
        name="pin",
    )(*arrays)


def project(coef, own, other, c):
    rows = jnp.concatenate([own[c], other[c]], axis=0)
    return jnp.dot(coef, rows, preferred_element_type=F32)


def sums(shared, items, outs, name, before=(), coefs=None):
    table, fields, coef, chunks = shared
    moved = [fields]
    for key, adds in items:
        for array in [chunks[key][0]] + [array for array, row in adds]:
            if not any(array is known for known in moved):
                moved.append(array)

    def index(array):
        return [array is known for known in moved].index(True)

    first = [coef] if coefs is None else list(coefs)

    def kernel(table_ref, *refs):
        refs = refs[len(before) :]
        if coefs is None:
            rows = refs[0][...]
        else:
            rows = jnp.concatenate([refs[0][...], refs[1][9, :, :128]], axis=1)
        refs = refs[len(first) :]
        ins, results = refs[: len(moved)], refs[len(moved) :]
        results[len(outs)][...] = jnp.zeros(TOKEN, F32)
        if coefs is not None:
            results[-1][...] = rows
        for number, group in enumerate(outs):
            for position, item in enumerate(group):
                (half, dx, dy), adds = items[item]
                chunk, row = chunks[(half, dx, dy)]
                lanes = pl.ds(pl.multiple_of(table_ref[dx * 2 + dy] * NPE, NPE), NPE)
                own = ins[0].at[pl.ds(half * 3, 3), :, lanes]
                other = ins[index(chunk)].at[pl.ds(row * 3, 3)]
                for c in range(3):
                    total = project(rows, own, other, c)
                    for array, place_in in adds:
                        total = total + ins[index(array)][place_in, c].astype(F32)
                    results[number][position, c] = total.astype(BF)

    shapes = [bf16(len(group), *ITEM) for group in outs] + [jax.ShapeDtypeStruct(TOKEN, F32)]
    if coefs is not None:
        shapes.append(bf16(128, 256))
    return pl.pallas_call(
        kernel,
        in_specs=[pl.BlockSpec(memory_space=pltpu.SMEM)]
        + [pl.BlockSpec(memory_space=pl.ANY)] * len(before)
        + [INSIDE] * (len(first) + len(moved)),
        out_specs=[INSIDE] * len(shapes),
        out_shape=shapes,
        compiler_params=pltpu.CompilerParams(vmem_limit_bytes=16 * MIB),
        cost_estimate=TINY,
        name=name,
    )(table, *before, *first, *moved)


KG = 8
BLOCKS = 32 // KG + 1


def assemble_kernel(rows, table, out_modes, token, coef_ref, tables_ref, weight_ref, metric_ref, *refs):
    count = len(rows[1]) + len(rows[2])
    fields_ref, chunk_ref, *add_refs = refs[: count + 2]
    refs = refs[count + 2 :]
    lanes = pl.ds(pl.multiple_of(table[0] * NPE, NPE), NPE)
    fields_u, fields_b = [
        [fields_ref.at[pl.ds(3 * half, 3), :, lanes], chunk_ref.at[pl.ds(3 * rows[0][half], 3)]] for half in range(2)
    ]
    adds_u = [ref.at[row] for ref, row in zip(add_refs, rows[1])]
    adds_b = [ref.at[row] for ref, row in zip(add_refs[len(adds_u) :], rows[2])]
    keep_ref, send_ref, z_ref, g_ref, cb_ref, pick_k, pick_d = refs
    first = table[17] == 0

    def put(elem, step, block):
        sides = block.reshape(8, 2, 8, 128)
        keep_ref[elem, :, step] = jnp.where(first, sides[:, 0], sides[:, 1]).astype(BF)
        send_ref[elem, :, step] = jnp.where(first, sides[:, 1], sides[:, 0]).astype(BF)

    half_weight = 0.5 * weight_ref[...]

    columns = lax.broadcasted_iota(jnp.int32, (1, 128), 1)
    pick_d[...] = jnp.zeros((128, 128), F32)
    for k in range(32):
        hot = (columns == out_modes[k]).astype(F32)
        pick_k[k : k + 1, :] = hot
        row = (k // 4) * 16 + k % 4
        pick_d[row : row + 1, :] = hot
    chosen = pick_k[...].astype(BF)

    coef = coef_ref[...]
    for a in range(3):
        u = project(coef, *fields_u, a)
        for ref in adds_u:
            u = u + ref[a].astype(F32)
        b = project(coef, *fields_b, a)
        for ref in adds_b:
            b = b + ref[a].astype(F32)
        for sign, z in ((0, u + b), (1, u - b)):
            z = z.astype(BF)
            z_ref[sign, a * 128 : a * 128 + 128] = z
            picked = jnp.dot(chosen, z, preferred_element_type=F32) * half_weight
            for k in range(32):
                cb_ref[sign, a, k * 16 : k * 16 + 16, :] = jnp.broadcast_to(
                    picked[k : k + 1], (16, NPE)
                ).astype(BF)

    half = NPE // 2
    gram = None
    for sign in range(2):
        z = z_ref[sign]
        derived = []
        for r in range(2):
            block = tables_ref[:half, r * NPE : r * NPE + half]
            derived.append([
                jnp.dot(z[:, side * half : side * half + half], block, preferred_element_type=F32)
                for side in range(2)
            ])
        full = jnp.dot(z, tables_ref[:, 2 * NPE :], preferred_element_type=F32)
        derived.append([full[:, :half], full[:, half:]])
        for a in range(3):
            for b in range(3):
                sides = []
                for side in range(2):
                    lanes = slice(side * half, side * half + half)
                    grad = None
                    for r in range(3):
                        term = metric_ref[r, b : b + 1, lanes] * derived[r][side][a * 128 : a * 128 + 128]
                        grad = term if grad is None else grad + term
                    sides.append(grad)
                grad = jnp.concatenate(sides, axis=1).astype(BF)
                g_ref[sign, a, b] = grad
                weighted = (grad.astype(F32) * half_weight).astype(BF)
                term = lax.dot_general(
                    grad, weighted, (((1,), (1,)), ((), ())), preferred_element_type=F32
                )
                gram = term if gram is None else gram + term
    diffusion = lax.dot_general(
        gram.astype(BF), pick_d[...].astype(BF), (((1,), (1,)), ((), ())), preferred_element_type=F32
    )
    for elem in range(8):
        put(elem, BLOCKS - 1, diffusion)
    group = lax.broadcasted_iota(jnp.int32, (128, 128), 1) // 16

    def rows_of(step):
        total = None
        for sign in range(2):
            for b in range(3):
                pieces = []
                for t in range(KG):
                    start = (step * KG + t) * 16
                    product = None
                    for a in range(3):
                        picked = cb_ref[sign, a, pl.ds(start, 16), :][None]
                        term = g_ref[sign, a, b].reshape(8, 16, NPE) * picked
                        product = term if product is None else product + term
                    pieces.append(product.reshape(128, NPE))
                modes = z_ref[1 - sign, b * 128 : b * 128 + 128]
                term = lax.dot_general(
                    jnp.concatenate(pieces, axis=0), modes, (((1,), (1,)), ((), ())), preferred_element_type=F32
                )
                total = term if total is None else total + term
        turned = [total[:128]] + [
            pltpu.roll(total[t * 128 : t * 128 + 128], 16 * t, 1) for t in range(1, KG)
        ]
        for elem in range(8):
            block = turned[0]
            for t in range(1, KG):
                block = jnp.where(group == (elem + t) % 8, turned[t], block)
            put(elem, step, block)

    for step in range(32 // KG):
        rows_of(step)


def assemble(shared, out_modes, tables, weights, metric, adds_u, adds_b, token):
    table, fields, coef, chunks = shared

    adds = adds_u + adds_b
    (chunk, row_u), (same, row_b) = chunks[(0, 0, 0)], chunks[(1, 0, 0)]
    rows = ((row_u, row_b), [row for array, row in adds_u], [row for array, row in adds_b])

    def kernel(*args):
        assemble_kernel(rows, *args)

    out = bf16(8, 8, BLOCKS, 8, 128)
    return pl.pallas_call(
        kernel,
        grid_spec=pltpu.PrefetchScalarGridSpec(
            num_scalar_prefetch=2,
            grid=(1,),
            in_specs=[
                pl.BlockSpec(memory_space=pl.ANY),
                whole((128, 256)),
                whole(tables.shape),
                pl.BlockSpec((1, NPE), lambda i, table, chosen: (0, table[0])),
                pl.BlockSpec((3, 3, NPE), lambda i, table, chosen: (0, 0, table[0])),
            ]
            + [INSIDE] * (2 + len(adds)),
            out_specs=[INSIDE] * 2,
            scratch_shapes=[
                pltpu.VMEM((2, 384, NPE), BF),
                pltpu.VMEM((2, 3, 3, 128, NPE), BF),
                pltpu.VMEM((2, 3, 512, NPE), BF),
                pltpu.VMEM((32, 128), F32),
                pltpu.VMEM((128, 128), F32),
            ],
        ),
        out_shape=[out] * 2,
        compiler_params=pltpu.CompilerParams(vmem_limit_bytes=32 * MIB),
        cost_estimate=TINY,
        name="assemble",
    )(table, out_modes, token, coef, tables, weights, metric, fields, chunk,
      *[array for array, row in adds])


def add_kernel(keep_ref, got_ref, out_ref):
    out_ref[...] = (keep_ref[...].astype(F32) + got_ref[...].astype(F32)).astype(BF)


def add(keep, got):
    return pl.pallas_call(
        add_kernel,
        out_shape=bf16(*keep.shape),
        compiler_params=pltpu.CompilerParams(vmem_limit_bytes=12 * MIB),
        name="add",
    )(keep, got)


def finish_kernel(table, in_ref, tensor_ref, diffusion_ref):
    total = jnp.sum(in_ref[...].astype(F32), axis=0).reshape(BLOCKS * 8, 128)
    total = jnp.concatenate([total, jnp.zeros((128 - BLOCKS * 8, 128), F32)], axis=0)
    shift = lax.rem(128 - 16 * table[16], 128)
    turned = pltpu.roll(total, shift, 1).T
    lane = lax.broadcasted_iota(jnp.int32, (16, 128), 1) % 8
    for j in range(8):
        rows = None
        for t in range(8):
            part = turned[t * 16 : t * 16 + 16]
            if t != j:
                part = pltpu.roll(part, (t - j) % 128, 1)
            rows = part if rows is None else jnp.where(lane == t, part, rows)
        tensor_ref[j] = rows[:, :32]
    diffusion_ref[...] = turned[:4, 32:40]


def finish(table, shares):
    return pl.pallas_call(
        finish_kernel,
        in_specs=[pl.BlockSpec(memory_space=pltpu.SMEM), INSIDE],
        out_specs=[INSIDE] * 2,
        out_shape=[jax.ShapeDtypeStruct((8, 16, 32), F32), jax.ShapeDtypeStruct((4, 8), F32)],
        compiler_params=pltpu.CompilerParams(vmem_limit_bytes=12 * MIB),
        name="finish",
    )(table, shares)


def bf16(*shape):
    return jax.ShapeDtypeStruct(shape, BF)


def on_device(snapshots, coefficients, mass_weights, metric, out_modes):
    fields = snapshots.transpose(1, 0, 2)
    coefficients = coefficients.T
    snap, elem = lax.axis_index("snap"), lax.axis_index("elem")
    x, y_hi, core = snap // 4, (snap // 2) % 2, snap % 2
    slot = lax.iota(jnp.int32, TABLE)
    side = jnp.where(slot < 8, core, 1 - core)
    table = side * 8 + ((x + ((slot // 2) % 4) * (1 + 2 * side)) % 4) * 2 + (y_hi ^ (slot % 2))
    table = jnp.where(slot < 16, table, jnp.where(slot < 17, elem, core)).astype(jnp.int32)

    U, B = 0, 1
    chunks, token, rows = {}, jnp.zeros(TOKEN, F32), None

    def trade(groups, name, space, coef=None):
        nonlocal token
        *values, token = cut(table, fields, groups, "cut_" + name, space, token, coef)
        for value, group in zip(values, groups):
            got = send(value, CORE, name)
            for row, key in enumerate(group):
                chunks[key] = (got, row)

    def total(items, outs, name, *before):
        nonlocal token, rows
        coefs = (coefficients, chunks[(B, 2, 1)][0]) if rows is None else None
        result = sums((table, fields, rows, chunks), items, outs, name, (token,) + before, coefs)
        if coefs is not None:
            rows = result[-1]
        token = result[len(outs)]
        return result[: len(outs)]

    trade([[(B, 2, 1), (U, 2, 0), (U, 2, 1)]], "near", pltpu.HBM, coefficients)
    trade(
        [
            [(B, 1, 1), (B, 3, 1), (U, 3, 0), (U, 3, 1)],
            [(B, 2, 0), (B, 0, 1), (U, 1, 0), (U, 1, 1)],
            [(B, 1, 0), (B, 3, 0), (U, 0, 1), (U, 0, 0), (B, 0, 0)],
        ],
        "far", pl.ANY,
    )
    yb1, xa1 = total([((B, 2, 1), []), ((U, 2, 0), []), ((U, 2, 1), [])], [[0], [1, 2]], "first")
    yb1, xa1 = send(yb1, Y2, "yb1"), send(xa1, FORWARD, "xa1")
    yb2, xa2 = total(
        [((B, 1, 1), []), ((B, 3, 1), []), ((U, 3, 0), []), ((U, 3, 1), [])], [[0, 1], [2, 3]], "second"
    )
    yb2, xa2 = send(yb2, Y2, "yb2"), send(xa2, BACK, "xa2")
    xb1, xa3, yb3 = total(
        [((B, 2, 0), [(yb1, 0)]), ((U, 1, 0), [(xa1, 0)]), ((U, 1, 1), [(xa1, 1)]), ((B, 0, 1), [])],
        [[0], [1, 2], [3]], "third",
    )
    xb1, xa3, yb3 = send(xb1, FORWARD, "xb1"), send(xa3, FORWARD, "xa3"), send(yb3, Y2, "yb3")
    token = pin(token, xa2, yb2)
    (ya,) = total([((U, 0, 1), [(xa2, 1), (xa3, 1)])], [[0]], "fourth")
    ya = send(ya, Y2, "ya")
    xb3, xb2 = total([((B, 1, 0), [(yb2, 0), (xb1, 0)]), ((B, 3, 0), [(yb2, 1)])], [[0], [1]], "fifth")
    xb3, xb2 = send(xb3, FORWARD, "xb3"), send(xb2, BACK, "xb2")
    token = pin(token, ya)

    keep, shares = assemble(
        (table, fields, rows, chunks), out_modes, derivative_tables(GLL), mass_weights.reshape(1, -1), metric,
        [(xa2, 0), (xa3, 0), (ya, 0)],
        [(yb3, 0), (xb2, 0), (xb3, 0)],
        token,
    )
    shares = add(keep, send(shares, CORE, "shares")).reshape(64, BLOCKS, 8, 128)
    shares = lax.all_to_all(shares, AXES, 0, 0, axis_index_groups=SAME_CORE, tiled=True)
    tensor, diffusion = finish(table, shares)
    return tensor.transpose(2, 0, 1), diffusion


def solution(mesh):
    return jax.shard_map(
        on_device,
        mesh=mesh,
        in_specs=(P("snap", None, "elem"), P("snap", None), P("elem"), P(None, None, "elem"), P()),
        out_specs=(P(None, "snap", "elem"), P("elem", "snap")),
        check_vma=False,
    )
```
